32 devices in a mesh: dp: 2 (over x), expert: 16 (over z, y, core).
Axes of the slice: x: 2, y: 2, z: 4, core: 2. Of those that a mesh axis runs over, the one named last changes fastest.
Arguments:
- tokens: bfloat16 [2048, 3584], P('expert'), may hold values from -6 to 6
- cotangent: bfloat16 [2048, 3584], P('expert'), may hold values from -0.59765625 to 0.59765625
- route_ids: int32 [2048, 8], P('expert'), may hold values from 0 to 15, all different within a row; in each aligned block of 128 rows (0 to 127, 128 to 255, ...) at most 80 rows name the same one
- route_gates: float32 [2048, 8], P('expert'), may hold values from 0.02 to 0.5
- w_gate: bfloat16 [16, 1792, 3584], P('expert', 'dp'), may hold values from -0.09375 to 0.09375
- w_up: bfloat16 [16, 1792, 3584], P('expert', 'dp'), may hold values from -0.09375 to 0.09375
- w_down: bfloat16 [16, 1792, 3584], P('expert', 'dp'), may hold values from -0.125 to 0.125
Outputs:
- layer_out: bfloat16 [2048, 3584], P(('expert', 'dp'))
- gate_grad: float32 [2048, 8], P(('expert', 'dp'))
- grad_w_gate: bfloat16 [16, 1792, 3584], P('expert', 'dp')
- grad_w_up: bfloat16 [16, 1792, 3584], P('expert', 'dp')
- grad_w_down: bfloat16 [16, 1792, 3584], P('expert', 'dp')
The draws below stay inside these ranges and needn't reach their ends.
Inputs may be any that keep to these rules, and one draw needn't show every extreme that they name: `route_ids`: each row names 8 different experts. Within each aligned block of 128 rows (the tokens of one index of expert) no expert is named more than 80 times, a bound that some block reaches.
All inputs are finite; a program needn't handle non-finite values.
Results may differ from the reference program's by a relative error of at most 0.02.
Values may be sent and summed in bfloat16 or wider, within the bound.
A program may use at most 128 MiB of HBM per device.

```python
import math
import jax
import jax.numpy as jnp
import numpy as np
from jax import lax

D = 3584
H = 1792
TOPK = 8
TOK_GRP = 128
EXPERTS = 16
TOKENS = 2048
CAP = 80
N_DP = 2
N_EXPERT = 16


def block_levels(rng, extent, shards, least, top_value):
    factor_of = 1.0
    for axis_at, parts in shards:
        heights = jax.random.uniform(jax.random.fold_in(jax.random.fold_in(rng, 6), axis_at), (parts,), jnp.float32, least / len(shards), top_value / len(shards))
        factor_of = factor_of * jnp.repeat(jnp.exp(heights), extent[axis_at] // parts).reshape((-1,) + (1,) * (len(extent) - 1 - axis_at))
    return factor_of


def routed_block(own_key, own, number, rows, amount, top, reach, lean):
    sequence = jax.random.permutation(own_key, amount)
    heavy_load, ordinary = portions_of(amount, rows * top, reach, lean, True), portions_of(amount, rows * top, reach, lean, False)
    places = jnp.arange(amount)

    def named(lengths, offset_by):
        used = int((lengths > 0).sum())
        fixed = max(1, used // 4)
        shifted = fixed + (places - fixed + offset_by * (used - fixed)) % max(1, amount - fixed)
        return jnp.zeros((amount,), jnp.int32).at[sequence[jnp.where(places < fixed, places, shifted)]].set(jnp.asarray(lengths, jnp.int32))

    lengths = jnp.where(number % 4 == 0, named(heavy_load, number // 4), named(ordinary, number - number // 4 - 1))
    mixed = jax.random.permutation(jax.random.fold_in(own, 3), amount)
    donor, sink = mixed[0:amount // 2 * 2:2], mixed[1:amount // 2 * 2:2]
    margin = jnp.minimum(lengths[donor] - 1, reach - lengths[sink]) // 2
    margin = jnp.where((donor == sequence[0]) | (sink == sequence[0]) | (lengths[sink] == 0), 0, jnp.maximum(margin, 0))
    shifted = jax.random.randint(jax.random.fold_in(own, 4), (amount // 2,), 0, 1 << 20) % (margin + 1)
    lengths = lengths.at[donor].add(-shifted).at[sink].add(shifted)
    items = jnp.searchsorted(jnp.cumsum(lengths), jnp.arange(rows * top), side="right").astype(jnp.int32)
    grid = items.reshape(top, rows).T
    grid = grid[jax.random.permutation(jax.random.fold_in(own, 1), rows)]
    offset_by = jax.random.randint(jax.random.fold_in(own, 2), (rows, 1), 0, top)
    return jnp.take_along_axis(grid, (jnp.arange(top)[None, :] + offset_by) % top, axis=1)


def portions_of(number_of, total, reach, lean, full):
    loads = [(1 << 20) // math.isqrt(grade ** lean) + 1 for grade in range(1, number_of + 1)]
    largest = reach if full else min(reach, max(-(-total // number_of), total * loads[0] // sum(loads)))
    least = 1 if total - largest >= number_of - 1 else 0
    holding, surplus = [largest] + [least] * (number_of - 1), total - largest - least * (number_of - 1)
    while surplus > 0:
        free = [i for i in range(1, number_of) if holding[i] < largest] or [i for i in range(1, number_of) if holding[i] < reach]
        pool, budget = sum([loads[i] for i in free]), surplus
        for i in free:
            more = min(reach - holding[i], max(1, budget * loads[i] // pool), surplus)
            holding[i] = holding[i] + more
            surplus = surplus - more
    return np.array(holding)


def scatter_about(own_key, shape, scale, most, split=(), kind=jnp.bfloat16):
    result = scale * jax.random.normal(own_key, shape, jnp.float32)
    if split:
        result = result * block_levels(own_key, shape, split, -0.22, 0.18)
    return jnp.clip(result, -most, most).astype(kind)


def setup_inputs(seed: int = 0) -> dict:
    streams_of = jax.random.split(jax.random.key(seed), 8)
    tokens = scatter_about(streams_of[0], (TOKENS, D), 1.0, 6.0, ((0, 16),))
    cotangent = scatter_about(streams_of[1], (TOKENS, D), 0.1, 0.59765625, ((0, 16),))
    route_ids_keys = jax.random.split(jax.random.fold_in(streams_of[2], 1), TOKENS // TOK_GRP)
    route_ids_turns = jax.random.permutation(jax.random.fold_in(streams_of[2], 3), TOKENS // TOK_GRP)
    route_ids = jax.vmap(lambda own, number: routed_block(jax.random.fold_in(streams_of[2], 2), own, number, TOK_GRP, EXPERTS, TOPK, CAP, 2))(route_ids_keys, route_ids_turns).reshape((TOKENS, TOPK))
    route_gates = jnp.clip(jnp.exp(math.log(0.5) - 3.218876 * jax.random.uniform(streams_of[3], (TOKENS, TOPK), jnp.float32) ** block_levels(streams_of[3], (TOKENS, TOPK), ((0, 16),), -0.2, 0.2)), 0.02, 0.5)
    w_gate = scatter_about(streams_of[4], (EXPERTS, H, D), D ** -0.5, 0.09375, ((0, 16), (1, 2)))
    w_up = scatter_about(streams_of[5], (EXPERTS, H, D), D ** -0.5, 0.09375, ((0, 16), (1, 2)))
    w_down = scatter_about(streams_of[6], (EXPERTS, H, D), H ** -0.5, 0.125, ((0, 16), (1, 2)))
    return dict(tokens=tokens, cotangent=cotangent, route_ids=route_ids, route_gates=route_gates, w_gate=w_gate, w_up=w_up, w_down=w_down)


def reference(tokens, cotangent, route_ids, route_gates, w_gate, w_up, w_down):
    flat_ids = route_ids.reshape(-1)
    slot_total = flat_ids.shape[0]
    block_width = H // N_DP
    limit_rows = N_EXPERT * CAP
    rows_x = jnp.repeat(tokens, TOPK, axis=0)
    rows_cot = jnp.repeat(cotangent, TOPK, axis=0)
    scaled = (route_gates[:, :, None] * cotangent[:, None, :].astype(jnp.float32)).astype(jnp.bfloat16)
    scaled = scaled.reshape(slot_total, D)

    def per_expert(running, expert):
        y_acc, g_acc = running
        chosen = jnp.nonzero(flat_ids == expert, size=limit_rows, fill_value=slot_total)[0].astype(jnp.int32)
        rows_in = jnp.take(rows_x, chosen, axis=0, mode="fill", fill_value=0)
        rows_dy = jnp.take(scaled, chosen, axis=0, mode="fill", fill_value=0)
        rows_ct = jnp.take(rows_cot, chosen, axis=0, mode="fill", fill_value=0)
        gate_local = lax.dynamic_index_in_dim(w_gate, expert, 0, keepdims=False)
        up_local = lax.dynamic_index_in_dim(w_up, expert, 0, keepdims=False)
        down_local = lax.dynamic_index_in_dim(w_down, expert, 0, keepdims=False)
        gate_pre = jnp.dot(rows_in, gate_local.T, preferred_element_type=jnp.float32)
        up_pre = jnp.dot(rows_in, up_local.T, preferred_element_type=jnp.float32)
        sigma_gate = jax.nn.sigmoid(gate_pre)
        hidden = (gate_pre * sigma_gate * up_pre).astype(jnp.bfloat16)
        y_part = jnp.einsum(
            "rjh,jhd->rjd",
            hidden.reshape(limit_rows, N_DP, block_width).astype(jnp.float32),
            down_local.reshape(N_DP, block_width, D).astype(jnp.float32),
            precision=lax.Precision.HIGHEST,
        ).astype(jnp.bfloat16)
        y_sum = jnp.sum(y_part.astype(jnp.float32), axis=1)
        g_sum = jnp.sum(y_sum * rows_ct.astype(jnp.float32), axis=1)
        y_acc = y_acc.at[chosen].add(y_sum, mode="drop")
        g_acc = g_acc.at[chosen].add(g_sum, mode="drop")
        hidden_grad = jnp.dot(rows_dy, down_local.T, preferred_element_type=jnp.float32)
        grad_gate_pre = (hidden_grad * up_pre * sigma_gate * (1.0 + gate_pre * (1.0 - sigma_gate))).astype(jnp.bfloat16)
        grad_up_pre = (hidden_grad * gate_pre * sigma_gate).astype(jnp.bfloat16)
        grad_down = jnp.dot(hidden.T, rows_dy, preferred_element_type=jnp.float32).astype(jnp.bfloat16)
        grad_gate = jnp.dot(grad_gate_pre.T, rows_in, preferred_element_type=jnp.float32).astype(jnp.bfloat16)
        grad_up = jnp.dot(grad_up_pre.T, rows_in, preferred_element_type=jnp.float32).astype(jnp.bfloat16)
        return (y_acc, g_acc), (grad_gate, grad_up, grad_down)

    start_state = (jnp.zeros((slot_total, D), jnp.float32), jnp.zeros((slot_total,), jnp.float32))
    final_state, grads = lax.scan(per_expert, start_state, jnp.arange(N_EXPERT, dtype=jnp.int32))
    y_all, g_all = final_state
    y_tok = y_all.reshape(TOKENS, TOPK, D)
    layer_out = jnp.sum(route_gates[:, :, None] * y_tok, axis=1).astype(jnp.bfloat16)
    gate_grad = g_all.reshape(TOKENS, TOPK)
    return layer_out, gate_grad, grads[0], grads[1], grads[2]
```

```python
import jax
import jax.numpy as jnp
from jax import lax
from jax.sharding import PartitionSpec as P

BY_FEATURE = (((1,), (1,)), ((), ()))
BY_ROW = (((0,), (0,)), ((), ()))


def swap(a, axis, bits):
    size = lax.axis_size(axis)
    return lax.ppermute(a, axis, [(i, i ^ bits) for i in range(size)])


def collect(a):
    dp_count = lax.axis_size("dp")
    z_count = lax.axis_size("expert") // 4
    rows, width = a.shape
    a = jnp.stack([a] + [swap(a, "expert", 4 * z) for z in range(1, z_count)])
    first = a[:, None, None, None, : rows // 2]
    second = a[:, None, None, None, rows // 2 :]

    def along_y(b):
        return jnp.concatenate([b, swap(b, "expert", 2)], axis=1)

    def along_dp(b):
        return jnp.concatenate([b] + [swap(b, "dp", d) for d in range(1, dp_count)], axis=3)

    both = jnp.concatenate([along_y(along_dp(first)), along_dp(along_y(second))], axis=2)
    return both.reshape(2 * z_count, dp_count * rows, width)


def hand_back(a, rows):
    dp_count = lax.axis_size("dp")
    z_count = lax.axis_size("expert") // 4
    width = a.shape[-1]
    a = a.reshape(z_count, 2, 2, dp_count, rows // 2, width)

    def total(parts):
        return sum(p.astype(jnp.float32) for p in parts).astype(jnp.bfloat16)

    def along_y(b):
        return total([b[:, :1], swap(b[:, 1:], "expert", 2)])

    def along_dp(b):
        return total([b[:, :, :1]] + [swap(b[:, :, d : d + 1], "dp", d) for d in range(1, dp_count)])

    first = along_dp(along_y(a[:, :, 0]))
    second = along_y(along_dp(a[:, :, 1]))
    both = jnp.concatenate([first, second], axis=3).reshape(z_count, rows, width)
    return total([both[0]] + [swap(both[z], "expert", 4 * z) for z in range(1, z_count)])


def body(tokens, cotangent, route_ids, route_gates, w_gate, w_up, w_down):
    groups = lax.axis_size("expert")
    dp_count = lax.axis_size("dp")
    me = lax.axis_index("expert")
    part = lax.axis_index("dp")
    tok_rows, width = tokens.shape
    top_slots = route_ids.shape[1]
    cap_rows = min(tok_rows, dp_count * max(1, tok_rows * top_slots * 5 // (4 * groups * dp_count)))
    own_rows = tok_rows // dp_count
    near = groups // 2

    def share(a):
        return lax.dynamic_slice_in_dim(a, part * own_rows, own_rows, 0)

    experts = jnp.arange(groups, dtype=jnp.int32)
    named = route_ids[:, :, None] == experts[None, None, :]
    gates = jnp.sum(jnp.where(named, route_gates[:, :, None], 0.0), axis=1)
    gates = lax.all_gather(gates, "expert", tiled=True)

    block = jnp.arange(groups * dp_count, dtype=jnp.int32)
    partner = (block // dp_count ^ me) * dp_count + (block % dp_count ^ part)
    partner = (partner[:, None] == block[None, :])[:, :, None]

    def reorder(a):
        return jnp.sum(jnp.where(partner, a.reshape(1, -1, own_rows), 0.0), axis=1)

    def near_far(expert):
        a = jnp.sum(jnp.where(experts == expert, gates, 0.0), axis=1)
        a = reorder(a).reshape(near, 2, dp_count, 2, own_rows // 2)
        return a.transpose(1, 0, 3, 2, 4).reshape(2, near, tok_rows)

    upto = jnp.triu(jnp.ones((tok_rows, tok_rows), jnp.bfloat16))
    places = jnp.arange(cap_rows, dtype=jnp.float32)

    def slots(a):
        chosen = a > 0
        count = jnp.dot(chosen.astype(jnp.bfloat16), upto, preferred_element_type=jnp.float32)
        rank = jnp.where(chosen, count - 1.0, -1.0)
        return rank[..., None, :] == places[:, None]

    own_gates = near_far(me)
    own_pick = slots(own_gates)
    gate_slot = jnp.sum(jnp.where(own_pick, own_gates[:, :, None, :], 0.0), axis=3).reshape(-1, 1)
    pair_pick = slots(near_far(me ^ 1)[0])
    pick = jnp.concatenate([own_pick[0], pair_pick], axis=1).astype(jnp.bfloat16)

    def to_slots(a):
        a = collect(share(a))
        rows = jnp.einsum("gct,gtd->gcd", pick[:, cap_rows:], a, preferred_element_type=jnp.float32)
        sent = swap(rows.astype(jnp.bfloat16), "expert", 1)
        rows = jnp.einsum("gct,gtd->gcd", pick[:, :cap_rows], a, preferred_element_type=jnp.float32)
        return jnp.concatenate([rows.astype(jnp.bfloat16), sent]).reshape(-1, width)

    x = to_slots(tokens)
    cot = to_slots(cotangent)
    gate_pre = lax.dot_general(x, w_gate[0], BY_FEATURE, preferred_element_type=jnp.float32)
    up_pre = lax.dot_general(x, w_up[0], BY_FEATURE, preferred_element_type=jnp.float32)
    sigma = jax.nn.sigmoid(gate_pre)
    hidden = gate_pre * sigma * up_pre
    scaled_hidden = (hidden * gate_slot).astype(jnp.bfloat16)

    y = jnp.dot(scaled_hidden, w_down[0], preferred_element_type=jnp.float32).astype(jnp.bfloat16)
    y = y.reshape(2, near, cap_rows, width)
    y = jnp.concatenate([y[0], swap(y[1], "expert", 1)], axis=1)
    y = jnp.einsum("gct,gcd->gtd", pick, y, preferred_element_type=jnp.float32)
    layer_out = hand_back(y.astype(jnp.bfloat16), own_rows)

    back = lax.dot_general(cot, w_down[0], BY_FEATURE, preferred_element_type=jnp.float32)
    slot_dot = jnp.sum(hidden * back, axis=1).reshape(2, near, cap_rows, 1)
    back = back * gate_slot
    grad_gate_pre = (back * up_pre * sigma * (1.0 + gate_pre * (1.0 - sigma))).astype(jnp.bfloat16)
    grad_up_pre = (back * gate_pre * sigma).astype(jnp.bfloat16)

    tok_dot = jnp.sum(jnp.where(own_pick, slot_dot, 0.0), axis=2)
    tok_dot = tok_dot.reshape(2, near, 2, dp_count, own_rows // 2).transpose(1, 0, 3, 2, 4)
    tok_dot = reorder(tok_dot).reshape(-1, 1)
    tok_dot = jnp.where(experts == me, tok_dot, 0.0)
    tok_dot = lax.psum_scatter(tok_dot, ("expert", "dp"), scatter_dimension=0, tiled=True)
    gate_grad = jnp.sum(jnp.where(share(named), tok_dot[:, None, :], 0.0), axis=2)

    grad_down = lax.dot_general(scaled_hidden, cot, BY_ROW, preferred_element_type=jnp.float32)
    grad_gate = lax.dot_general(grad_gate_pre, x, BY_ROW, preferred_element_type=jnp.float32)
    grad_up = lax.dot_general(grad_up_pre, x, BY_ROW, preferred_element_type=jnp.float32)
    return (
        layer_out,
        gate_grad,
        grad_gate.astype(jnp.bfloat16)[None],
        grad_up.astype(jnp.bfloat16)[None],
        grad_down.astype(jnp.bfloat16)[None],
    )


def solution(mesh):
    return jax.shard_map(
        body,
        mesh=mesh,
        in_specs=(
            P("expert", None),
            P("expert", None),
            P("expert", None),
            P("expert", None),
            P("expert", "dp", None),
            P("expert", "dp", None),
            P("expert", "dp", None),
        ),
        out_specs=(
            P(("expert", "dp"), None),
            P(("expert", "dp"), None),
            P("expert", "dp", None),
            P("expert", "dp", None),
            P("expert", "dp", None),
        ),
        check_vma=False,
    )
```

```python
import jax
import jax.numpy as jnp
from jax import lax
from jax.sharding import PartitionSpec as P

BY_FEATURE = (((1,), (1,)), ((), ()))
BY_ROW = (((0,), (0,)), ((), ()))


def swap(a, axis, bits):
    size = lax.axis_size(axis)
    return lax.ppermute(a, axis, [(i, i ^ bits) for i in range(size)])


def collect(a, after=None):
    dp_count = lax.axis_size("dp")
    z_count = lax.axis_size("expert") // 4
    rows, width = a.shape
    if after is not None:
        a, _ = lax.optimization_barrier((a, after))
    a = jnp.stack([a] + [swap(a, "expert", 4 * z) for z in range(1, z_count)])
    first = a[:, None, None, None, : rows // 2]
    second = a[:, None, None, None, rows // 2 :]

    def along_y(b):
        return jnp.concatenate([b, swap(b, "expert", 2)], axis=1)

    def along_dp(b):
        return jnp.concatenate([b] + [swap(b, "dp", d) for d in range(1, dp_count)], axis=3)

    both = jnp.concatenate([along_y(along_dp(first)), along_dp(along_y(second))], axis=2)
    return both.reshape(2 * z_count, dp_count * rows, width), a


def hand_back(a, rows):
    dp_count = lax.axis_size("dp")
    z_count = lax.axis_size("expert") // 4
    width = a.shape[-1]
    a = a.reshape(z_count, 2, 2, dp_count, rows // 2, width)

    def total(parts):
        return sum(p.astype(jnp.float32) for p in parts).astype(jnp.bfloat16)

    def along_y(b):
        return total([b[:, :1], swap(b[:, 1:], "expert", 2)])

    def along_dp(b):
        return total([b[:, :, :1]] + [swap(b[:, :, d : d + 1], "dp", d) for d in range(1, dp_count)])

    first = along_dp(along_y(a[:, :, 0]))
    second = along_y(along_dp(a[:, :, 1]))
    both = jnp.concatenate([first, second], axis=3).reshape(z_count, rows, width)
    return total([both[0]] + [swap(both[z], "expert", 4 * z) for z in range(1, z_count)])


def body(tokens, cotangent, route_ids, route_gates, w_gate, w_up, w_down):
    groups = lax.axis_size("expert")
    dp_count = lax.axis_size("dp")
    me = lax.axis_index("expert")
    part = lax.axis_index("dp")
    tok_rows, width = tokens.shape
    top_slots = route_ids.shape[1]
    cap_rows = min(tok_rows, dp_count * max(1, tok_rows * top_slots * 5 // (4 * groups * dp_count)))
    own_rows = tok_rows // dp_count
    near = groups // 2

    def share(a):
        return lax.dynamic_slice_in_dim(a, part * own_rows, own_rows, 0)

    experts = jnp.arange(groups, dtype=jnp.int32)
    named = route_ids[:, :, None] == experts[None, None, :]
    gates = jnp.sum(jnp.where(named, route_gates[:, :, None], 0.0), axis=1)
    gates = gates.T
    gates = jnp.stack([gates, gates[experts ^ 1]], axis=1)
    gates = lax.all_to_all(gates, "expert", split_axis=0, concat_axis=0, tiled=True)

    block = jnp.arange(groups * dp_count, dtype=jnp.int32)
    partner = (block // dp_count ^ me) * dp_count + (block % dp_count ^ part)
    partner = (partner[:, None] == block[None, :])[:, :, None]

    def reorder(a):
        return jnp.sum(jnp.where(partner, a.reshape(1, -1, own_rows), 0.0), axis=1)

    def near_far(a):
        a = reorder(a).reshape(near, 2, dp_count, 2, own_rows // 2)
        return a.transpose(1, 0, 3, 2, 4).reshape(2, near, tok_rows)

    upto = jnp.triu(jnp.ones((tok_rows, tok_rows), jnp.bfloat16))
    places = jnp.arange(cap_rows, dtype=jnp.float32)

    def slots(a):
        chosen = a > 0
        count = jnp.dot(chosen.astype(jnp.bfloat16), upto, preferred_element_type=jnp.float32)
        rank = jnp.where(chosen, count - 1.0, -1.0)
        return rank[..., None, :] == places[:, None]

    own_gates = near_far(gates[:, 0])
    own_pick = slots(own_gates)
    gate_slot = jnp.sum(jnp.where(own_pick, own_gates[:, :, None, :], 0.0), axis=3).reshape(-1, 1)
    pair_pick = slots(near_far(gates[:, 1])[0])
    pick = jnp.concatenate([own_pick[0], pair_pick], axis=1).astype(jnp.bfloat16)

    def to_slots(a):
        rows = jnp.einsum("gct,gtd->gcd", pick[:, cap_rows:], a, preferred_element_type=jnp.float32)
        sent = swap(rows.astype(jnp.bfloat16), "expert", 1)
        rows = jnp.einsum("gct,gtd->gcd", pick[:, :cap_rows], a, preferred_element_type=jnp.float32)
        return jnp.concatenate([rows.astype(jnp.bfloat16), sent]).reshape(-1, width)

    all_x, column = collect(share(tokens), gates)
    all_cot, _ = collect(share(cotangent), column)
    x = to_slots(all_x)
    cot = to_slots(all_cot)
    gate_pre = lax.dot_general(x, w_gate[0], BY_FEATURE, preferred_element_type=jnp.float32)
    up_pre = lax.dot_general(x, w_up[0], BY_FEATURE, preferred_element_type=jnp.float32)
    sigma = jax.nn.sigmoid(gate_pre)
    hidden = gate_pre * sigma * up_pre
    scaled_hidden = (hidden * gate_slot).astype(jnp.bfloat16)

    y = jnp.dot(scaled_hidden, w_down[0], preferred_element_type=jnp.float32).astype(jnp.bfloat16)
    y = y.reshape(2, near, cap_rows, width)
    y = jnp.concatenate([y[0], swap(y[1], "expert", 1)], axis=1)
    y = jnp.einsum("gct,gcd->gtd", pick, y, preferred_element_type=jnp.float32)
    layer_out = hand_back(y.astype(jnp.bfloat16), own_rows)

    back = lax.dot_general(cot, w_down[0], BY_FEATURE, preferred_element_type=jnp.float32)
    slot_dot = jnp.sum(hidden * back, axis=1).reshape(2, near, cap_rows, 1)
    back = back * gate_slot
    grad_gate_pre = (back * up_pre * sigma * (1.0 + gate_pre * (1.0 - sigma))).astype(jnp.bfloat16)
    grad_up_pre = (back * gate_pre * sigma).astype(jnp.bfloat16)

    tok_dot = jnp.sum(jnp.where(own_pick, slot_dot, 0.0), axis=2)
    tok_dot = tok_dot.reshape(2, near, 2, dp_count, own_rows // 2).transpose(1, 0, 3, 2, 4)
    tok_dot = reorder(tok_dot)
    tok_dot = lax.all_to_all(tok_dot, ("expert", "dp"), split_axis=0, concat_axis=0, tiled=True)
    tok_dot = jnp.sum(tok_dot.reshape(groups, dp_count, own_rows), axis=1)
    gate_grad = jnp.sum(jnp.where(share(named), tok_dot.T[:, None, :], 0.0), axis=2)

    grad_down = lax.dot_general(scaled_hidden, cot, BY_ROW, preferred_element_type=jnp.float32)
    grad_gate = lax.dot_general(grad_gate_pre, x, BY_ROW, preferred_element_type=jnp.float32)
    grad_up = lax.dot_general(grad_up_pre, x, BY_ROW, preferred_element_type=jnp.float32)
    return (
        layer_out,
        gate_grad,
        grad_gate.astype(jnp.bfloat16)[None],
        grad_up.astype(jnp.bfloat16)[None],
        grad_down.astype(jnp.bfloat16)[None],
    )


def solution(mesh):
    return jax.shard_map(
        body,
        mesh=mesh,
        in_specs=(
            P("expert", None),
            P("expert", None),
            P("expert", None),
            P("expert", None),
            P("expert", "dp", None),
            P("expert", "dp", None),
            P("expert", "dp", None),
        ),
        out_specs=(
            P(("expert", "dp"), None),
            P(("expert", "dp"), None),
            P("expert", "dp", None),
            P("expert", "dp", None),
            P("expert", "dp", None),
        ),
        check_vma=False,
    )
```
